32 devices in a mesh: tok: 8 (over z, core), tp: 4 (over y, x).
Axes of the slice: x: 2, y: 2, z: 4, core: 2. Of those that a mesh axis runs over, the one named last changes fastest.
Arguments:
- hidden_states: bfloat16 [16384, 1024], P(('tok', 'tp')), may hold values from -40 to 40
- first_gain: float32 [1024], replicated, may hold values from 0.1 to 1.9
- second_gain: float32 [1024], replicated, may hold values from 0.1 to 1.9
- w_query: bfloat16 [1024, 1024], P(None, 'tp'), may hold values from -1 to 1
- w_keyval: bfloat16 [1024, 1024], replicated, may hold values from -0.375 to 0.375
- w_out: bfloat16 [1024, 1024], P('tp'), may hold values from -0.75 to 0.75
- kv_cache: bfloat16 [192, 128, 1024], P('tok'), may hold values from -310 to 310
- page_table: int32 [16, 16], P('tok'), may hold values from 0 to 191, as said below
- cached_len: int32 [16], P('tok'), may hold values from 128 to 2048, as said below
- expert_ids: int32 [16384, 8], P(('tok', 'tp')), may hold values from 0 to 31, all different within a row; in each aligned block of 512 rows (0 to 511, 512 to 1023, ...) at most 256 rows name the same one
- gate_weights: float32 [16384, 8], P(('tok', 'tp')), may hold values from 0.1 to 1
- w_gate_up: bfloat16 [32, 1024, 1024], P('tp', 'tok'), may hold values from -0.1875 to 0.1875
- w_down: bfloat16 [32, 512, 1024], P('tp', 'tok'), may hold values from -1 to 1
Outputs:
- layer_out: bfloat16 [16384, 1024], P(('tok', 'tp'))
The draws below stay inside these ranges and needn't reach their ends.
Inputs may be any that keep to these rules, and one draw needn't show every extreme that they name: `page_table`: request r's entries are pages of its own tok index, rows 24 * (r // 2) to 24 * (r // 2 + 1) - 1; its first 8 entries are the same for all requests of that tok index, and all other entries name pages that no other entry names. `cached_len`: some request has exactly 2048 cached tokens. `expert_ids`: in the rows of one device (aligned blocks of 512 rows) no expert is named by more than 256 rows, and a row names 8 different experts.
All inputs are finite; a program needn't handle non-finite values.
Results may differ from the reference program's by a relative error of at most 0.017.
The reference program's roundings to bfloat16 on the way count: a program that leaves them out, or rounds other values in their place, can miss the bound.
Values may be sent and summed in bfloat16 or wider, within the bound.
A program may use at most 128 MiB of HBM per device.

```python
import math
import jax
import jax.numpy as jnp
import numpy as np
from jax import lax

D = 1024
HEADS = 16
KV_HEADS = 8
HEAD_DIM = 64
EXPERTS = 32
FF_EXPERT = 512
TOP = 8
PAGE = 128
NEW = 1024
MAX_CACHED = 2048
SHARED_PAGES = 8
REQ_DEV = 2
REQUESTS = 16
TOKENS = 16384
TOK_DEV = 512
CAPACITY = 256
MAX_PAGES = 16
POOL_DEV = 24
POOL = 192


def table_pages(key):
    groups = REQUESTS // REQ_DEV
    group_keys = jax.random.split(jax.random.fold_in(key, 7), groups)

    def one_order(group_key):
        return jax.random.permutation(group_key, POOL_DEV)
    orders = jax.vmap(one_order)(group_keys)
    request_ids = jnp.arange(REQUESTS)
    group_of = request_ids // REQ_DEV
    within = request_ids % REQ_DEV
    page_pos = jnp.arange(MAX_PAGES)
    slot_ids = jnp.where(page_pos[None, :] < SHARED_PAGES, page_pos[None, :], SHARED_PAGES + within[:, None] * (MAX_PAGES - SHARED_PAGES) + page_pos[None, :] - SHARED_PAGES)
    return group_of[:, None] * POOL_DEV + orders[group_of[:, None], slot_ids]


def draw_page_table(key, part):
    return table_pages(key).astype(jnp.int32)


def draw_cached_len(key, part):
    lengths = jax.random.randint(jax.random.fold_in(key, 11), (REQUESTS,), PAGE, MAX_CACHED + 1)
    longest = jax.random.randint(jax.random.fold_in(key, 13), (), 0, REQUESTS)
    return jnp.where(jnp.arange(REQUESTS) == longest, MAX_CACHED, lengths).astype(jnp.int32)


def draw_kv_cache(key, part):
    base_key = jax.random.fold_in(jax.random.fold_in(key, 3), 0)
    shape = (POOL, PAGE, 2 * KV_HEADS * HEAD_DIM)
    cache = jax.random.truncated_normal(base_key, -6.0, 6.0, shape, jnp.float32) * 2.0
    return cache.astype(jnp.bfloat16)


def draw_hidden_states(key, part):
    noise_key, row_key, column_key = jax.random.split(jax.random.fold_in(key, 5), 3)
    row_scale = jnp.exp(jax.random.uniform(row_key, (TOKENS, 1), jnp.float32, -1.1513, 1.1513))
    column_scale = jnp.exp(jax.random.uniform(column_key, (1, D), jnp.float32, -1.1513, 1.1513))
    values = jax.random.truncated_normal(noise_key, -4.0, 4.0, (TOKENS, D), jnp.float32)
    return (values * row_scale * column_scale).astype(jnp.bfloat16)


def shard_levels(rng, shape, pieces, low, largest):
    def one(axis_at, parts):
        draws = jax.random.uniform(jax.random.fold_in(jax.random.fold_in(rng, 6), axis_at), (parts,), jnp.float32, low / len(pieces), largest / len(pieces))
        return jnp.repeat(jnp.exp(draws), shape[axis_at] // parts).reshape((-1,) + (1,) * (len(shape) - axis_at - 1))

    level = one(*pieces[0])
    for cut in pieces[1:]:
        level = level * one(*cut)
    return level


def deal_out(stream_key, own, number, rows, count, top, most, lean):
    sequence = jax.random.permutation(stream_key, count)
    crowded, usual = load_shares(count, rows * top, most, lean, True), load_shares(count, rows * top, most, lean, False)
    places = jnp.arange(count)

    def named(sizes, turn):
        used = int((sizes > 0).sum())
        fixed = max(1, used // 4)
        passed = fixed + (places - fixed + turn * (used - fixed)) % max(1, count - fixed)
        return jnp.zeros((count,), jnp.int32).at[sequence[jnp.where(places < fixed, places, passed)]].set(jnp.asarray(sizes, jnp.int32))

    sizes = jnp.where(number % 4 == 0, named(crowded, number // 4), named(usual, number - number // 4 - 1))
    mixed = jax.random.permutation(jax.random.fold_in(own, 3), count)
    giver, taker = mixed[0:count // 2 * 2:2], mixed[1:count // 2 * 2:2]
    margin = jnp.minimum(sizes[giver] - 1, most - sizes[taker]) // 2
    margin = jnp.where((giver == sequence[0]) | (taker == sequence[0]) | (sizes[taker] == 0), 0, jnp.maximum(margin, 0))
    passed = jax.random.randint(jax.random.fold_in(own, 4), (count // 2,), 0, 1 << 20) % (margin + 1)
    sizes = sizes.at[giver].add(-passed).at[taker].add(passed)
    labels = jnp.searchsorted(jnp.cumsum(sizes), jnp.arange(rows * top), side="right").astype(jnp.int32)
    table = labels.reshape(top, rows).T
    table = table[jax.random.permutation(jax.random.fold_in(own, 1), rows)]
    turn = jax.random.randint(jax.random.fold_in(own, 2), (rows, 1), 0, top)
    return jnp.take_along_axis(table, (jnp.arange(top)[None, :] + turn) % top, axis=1)


def load_shares(number_of, total, reach, skew, full):
    portions = [(1 << 20) // math.isqrt(rank ** skew) + 1 for rank in range(1, number_of + 1)]
    largest = reach if full else min(reach, max(-(-total // number_of), total * portions[0] // sum(portions)))
    least = 1 if total - largest >= number_of - 1 else 0
    given, spare = [largest] + [least] * (number_of - 1), total - largest - least * (number_of - 1)
    while spare > 0:
        candidates = [i for i in range(1, number_of) if given[i] < largest] or [i for i in range(1, number_of) if given[i] < reach]
        mass, left = sum([portions[i] for i in candidates]), spare
        for i in candidates:
            more = min(reach - given[i], max(1, left * portions[i] // mass), spare)
            given[i] = given[i] + more
            spare = spare - more
    return np.array(given)


def centred(rng, shape, deviation, limit, pieces=(), held_as=jnp.bfloat16):
    result = jax.random.normal(rng, shape, jnp.float32) * deviation
    if len(pieces) > 0:
        result = shard_levels(rng, shape, pieces, -0.22, 0.18) * result
    return jnp.clip(result, min=-limit, max=limit).astype(held_as)


def setup_inputs(seed: int = 0) -> dict:
    key_list = jax.random.split(jax.random.key(seed), 14)
    hidden_states = draw_hidden_states(jax.random.fold_in(key_list[13], 71), 0)
    first_gain = jnp.clip(1.0 + 0.18 * jax.random.normal(key_list[1], (D,), jnp.float32), 0.1, 1.9)
    second_gain = jnp.clip(1.0 + 0.18 * jax.random.normal(key_list[2], (D,), jnp.float32), 0.1, 1.9)
    w_query = centred(key_list[3], (D, HEADS * HEAD_DIM), (D // 32) ** -0.5, 1.0, ((1, 4),))
    w_keyval = centred(key_list[4], (D, 2 * KV_HEADS * HEAD_DIM), (D // 4) ** -0.5, 0.375)
    w_out = centred(key_list[5], (HEADS * HEAD_DIM, D), (HEADS * HEAD_DIM // 16) ** -0.5, 0.75, ((0, 4),))
    kv_cache = draw_kv_cache(jax.random.fold_in(key_list[13], 71), 0)
    page_table = draw_page_table(jax.random.fold_in(key_list[13], 71), 0)
    cached_len = draw_cached_len(jax.random.fold_in(key_list[13], 71), 0)
    expert_ids_keys = jax.random.split(jax.random.fold_in(key_list[9], 1), TOKENS // TOK_DEV)
    expert_ids_turns = jax.random.permutation(jax.random.fold_in(key_list[9], 3), TOKENS // TOK_DEV)
    expert_ids = jax.vmap(lambda own, number: deal_out(jax.random.fold_in(key_list[9], 2), own, number, TOK_DEV, EXPERTS, TOP, CAPACITY, 2))(expert_ids_keys, expert_ids_turns).reshape((TOKENS, TOP))
    gate_weights = jnp.clip(jnp.exp(math.log(1.0) - 2.3025851 * jax.random.uniform(key_list[10], (TOKENS, TOP), jnp.float32) ** shard_levels(key_list[10], (TOKENS, TOP), ((0, 32),), -0.2, 0.2)), 0.1, 1.0)
    w_gate_up = centred(key_list[11], (EXPERTS, D, 2 * FF_EXPERT), D ** -0.5, 0.1875, ((0, 4), (1, 8)))
    w_down = centred(key_list[12], (EXPERTS, FF_EXPERT, D), (FF_EXPERT // 16) ** -0.5, 1.0, ((0, 4), (1, 8)))
    return {"hidden_states": hidden_states, "first_gain": first_gain, "second_gain": second_gain, "w_query": w_query, "w_keyval": w_keyval, "w_out": w_out, "kv_cache": kv_cache, "page_table": page_table, "cached_len": cached_len, "expert_ids": expert_ids, "gate_weights": gate_weights, "w_gate_up": w_gate_up, "w_down": w_down}


ATTN_SCALE = 0.015625
EPSILON = 1e-06
THETA = 10000.0

def rms_norm(values, gain):
    wide = values.astype(jnp.float32)
    factor = lax.rsqrt(lax.optimization_barrier(jnp.mean(wide * wide, axis=-1, keepdims=True)) + EPSILON)
    return (wide * factor * gain).astype(jnp.bfloat16)

def rotate(values, positions):
    row_count = values.shape[0]
    shaped = values.reshape(row_count, -1, HEAD_DIM)
    half_dim = HEAD_DIM // 2
    exponent = jnp.arange(half_dim).astype(jnp.float32) * (2.0 / HEAD_DIM)
    frequency = jnp.power(THETA, -exponent)
    angles = positions.astype(jnp.float32)[:, None] * frequency[None, :]
    cosine = jnp.cos(angles)[:, None, :]
    sine_part = jnp.sin(angles)[:, None, :]
    leading = shaped[..., :half_dim]
    trailing = shaped[..., half_dim:]
    turned = jnp.concatenate([leading * cosine - trailing * sine_part, trailing * cosine + leading * sine_part], axis=-1)
    return turned.reshape(row_count, -1)

def attend_request(queries, keys_total, values_total, length):
    block_rows = min(NEW, 512)
    key_index = jnp.arange(MAX_CACHED + NEW).astype(jnp.int32)
    keys_wide = keys_total.astype(jnp.float32)
    values_wide = values_total.astype(jnp.float32)

    def one_block(block_start):
        block_query = lax.dynamic_slice_in_dim(queries, block_start, block_rows, 0).astype(jnp.float32)
        scores = jnp.einsum('qgpd,kgd->gpqk', block_query, keys_wide) * ATTN_SCALE
        query_pos = block_start + jnp.arange(block_rows).astype(jnp.int32)
        allowed = jnp.where(key_index[None, :] < MAX_CACHED, key_index[None, :] < length, key_index[None, :] - MAX_CACHED <= query_pos[:, None])
        scores = jnp.where(allowed, scores, -1e+30)
        top_score = lax.optimization_barrier(jnp.max(scores, axis=-1, keepdims=True))
        weights = jnp.exp(scores - top_score)
        probs = (weights / lax.optimization_barrier(jnp.sum(weights, axis=-1, keepdims=True))).astype(jnp.bfloat16)
        mixed = jnp.einsum('gpqk,kgd->qgpd', probs.astype(jnp.float32), values_wide)
        return mixed.astype(jnp.bfloat16).reshape(block_rows, -1)
    starts = jnp.arange(NEW // block_rows).astype(jnp.int32) * block_rows
    return lax.map(one_block, starts).reshape(NEW, -1)

def reference(hidden_states, first_gain, second_gain, w_query, w_keyval, w_out, kv_cache, page_table, cached_len, expert_ids, gate_weights, w_gate_up, w_down):
    group_size = HEADS // KV_HEADS
    kv_cols = KV_HEADS * HEAD_DIM
    normed = rms_norm(hidden_states, first_gain)
    positions = (cached_len[:, None] + jnp.arange(NEW).astype(jnp.int32)[None, :]).reshape(-1)
    queries = rotate(jnp.dot(normed, w_query, preferred_element_type=jnp.float32), positions).astype(jnp.bfloat16)
    keyval = jnp.dot(normed, w_keyval, preferred_element_type=jnp.float32)
    new_keys = rotate(keyval[:, :kv_cols], positions).astype(jnp.bfloat16)
    new_values = keyval[:, kv_cols:].astype(jnp.bfloat16)

    def per_request(inputs):
        page_ids, length, request_q, request_k, request_v = inputs
        cached = kv_cache[page_ids].reshape(MAX_CACHED, 2 * kv_cols)
        keys_total = jnp.concatenate([cached[:, :kv_cols], request_k], axis=0).reshape(MAX_CACHED + NEW, KV_HEADS, HEAD_DIM)
        values_total = jnp.concatenate([cached[:, kv_cols:], request_v], axis=0).reshape(MAX_CACHED + NEW, KV_HEADS, HEAD_DIM)
        return attend_request(request_q.reshape(NEW, KV_HEADS, group_size, HEAD_DIM), keys_total, values_total, length)
    attended = lax.map(per_request, (page_table, cached_len, queries.reshape(REQUESTS, NEW, -1), new_keys.reshape(REQUESTS, NEW, -1), new_values.reshape(REQUESTS, NEW, -1)))
    attended = attended.reshape(TOKENS, HEADS * HEAD_DIM)
    projected = jnp.dot(attended, w_out, preferred_element_type=jnp.float32)
    middle = (hidden_states.astype(jnp.float32) + projected).astype(jnp.bfloat16)
    normed_two = rms_norm(middle, second_gain)
    bound = TOKENS // TOK_DEV * CAPACITY

    def per_expert(accum, expert):
        chosen = expert_ids == expert
        picked = jnp.any(chosen, axis=1)
        weight_row = lax.optimization_barrier(jnp.sum(jnp.where(chosen, gate_weights, 0.0), axis=1))
        row_ids = jnp.nonzero(picked, size=bound, fill_value=0)[0]
        valid = jnp.arange(bound) < jnp.sum(picked)
        rows_in = normed_two[row_ids]
        both = jnp.dot(rows_in, w_gate_up[expert], preferred_element_type=jnp.float32)
        activated = (jax.nn.silu(both[:, :FF_EXPERT]) * both[:, FF_EXPERT:]).astype(jnp.bfloat16)
        produced = jnp.dot(activated, w_down[expert], preferred_element_type=jnp.float32).astype(jnp.bfloat16)
        scaled = jnp.where(valid[:, None], weight_row[row_ids][:, None] * produced.astype(jnp.float32), 0.0)
        return (accum.at[row_ids].add(scaled), None)
    accum, unused = lax.scan(per_expert, jnp.zeros((TOKENS, D), jnp.float32), jnp.arange(EXPERTS).astype(jnp.int32))
    return (middle.astype(jnp.float32) + accum).astype(jnp.bfloat16)
```

```python
import functools

import jax
import jax.numpy as jnp
from jax import lax
from jax.experimental import pallas as pl
from jax.experimental.pallas import tpu as pltpu
from jax.sharding import PartitionSpec as P

D = 1024
HEADS = 16
KV_HEADS = 8
HEAD_DIM = 64
EXPERTS = 32
FF_EXPERT = 512
TOP = 8
NEW = 1024
REQ_DEV = 2
PAGE = 128
MAX_PAGES = 16

ATTN_SCALE = 0.015625
EPSILON = 1e-06
THETA = 10000.0

LANES = 128
PAIRS = KV_HEADS // 2
KEY_BLOCK = 512
EXPERT_GROUPS = 2
NEGATIVE = -1e30
VMEM_LIMIT = 56 * 1024 * 1024


def params(*semantics):
    return pltpu.CompilerParams(
        vmem_limit_bytes=VMEM_LIMIT, dimension_semantics=semantics or None
    )


def rms_rows(wide, gain):
    factor = lax.rsqrt(jnp.mean(wide * wide, axis=-1, keepdims=True) + EPSILON)
    return (wide * factor * gain).astype(jnp.bfloat16)


def turn(values, cosine, sine):
    lane = lax.broadcasted_iota(jnp.int32, values.shape, 1)
    partner = jnp.where(
        lane % HEAD_DIM < HEAD_DIM // 2, pltpu.roll(values, 96, 1), pltpu.roll(values, 32, 1)
    )
    return values * cosine + partner * sine


def keyval_kernel(x_ref, gain_ref, w_ref, cos_ref, sin_ref, normed_ref, kv_ref):
    normed = rms_rows(x_ref[...].astype(jnp.float32), gain_ref[...])
    normed_ref[...] = normed
    for at in range(0, D, 256):
        part = jnp.dot(normed, w_ref[:, at : at + 256], preferred_element_type=jnp.float32)
        for sub in range(0, 256, LANES):
            piece = part[:, sub : sub + LANES]
            if at < KV_HEADS * HEAD_DIM:
                piece = turn(piece, cos_ref[...], sin_ref[...])
            kv_ref[:, at + sub : at + sub + LANES] = piece.astype(jnp.bfloat16)


def query_kernel(normed_ref, w_ref, cos_ref, sin_ref, q_ref):
    normed = normed_ref[...]
    for at in range(0, D, 256):
        part = jnp.dot(normed, w_ref[:, at : at + 256], preferred_element_type=jnp.float32)
        for sub in range(0, 256, LANES):
            piece = turn(part[:, sub : sub + LANES], cos_ref[...], sin_ref[...])
            piece = piece.astype(jnp.bfloat16).astype(jnp.float32) * ATTN_SCALE
            q_ref[:, at + sub : at + sub + LANES] = piece.astype(jnp.bfloat16)


def attention_kernel(
    pages_ref, sizes_ref, q_ref, ck_ref, cv_ref, nk_ref, nv_ref, o_ref, qp, top, acc
):
    rows = q_ref.shape[0]
    length = sizes_ref[0]
    first_row = sizes_ref[1]
    lane = lax.broadcasted_iota(jnp.int32, (rows, LANES), 1)
    low = lane < HEAD_DIM
    for head in range(4):
        block = q_ref[:, (head // 2) * LANES : (head // 2 + 1) * LANES].astype(jnp.float32)
        if head in (1, 2):
            block = pltpu.roll(block, HEAD_DIM, 1)
        keep = low if head < 2 else jnp.logical_not(low)
        qp[head] = jnp.where(keep, block, 0.0).astype(jnp.bfloat16)
        top[head] = jnp.full((rows, 1), NEGATIVE, jnp.float32)
        acc[head] = jnp.zeros((rows, 2 * LANES), jnp.float32)

    def update(keys, values, allowed):
        extended = jnp.concatenate([values, jnp.ones_like(values)], axis=1)
        for head in range(4):
            scores = lax.dot_general(
                qp[head], keys, (((1,), (1,)), ((), ())), preferred_element_type=jnp.float32
            )
            if allowed is not None:
                scores = jnp.where(allowed, scores, NEGATIVE)
            before = top[head]
            after = jnp.maximum(before, jnp.max(scores, axis=1, keepdims=True))
            weights = jnp.exp(scores - after).astype(jnp.bfloat16)
            top[head] = after
            acc[head] = acc[head] * jnp.exp(before - after) + jnp.dot(
                weights, extended, preferred_element_type=jnp.float32
            )

    per_block = KEY_BLOCK // PAGE

    def cached_block(index):
        ids = [pages_ref[index * per_block + i] for i in range(per_block)]
        keys = jnp.concatenate([ck_ref[page] for page in ids], axis=0)
        values = jnp.concatenate([cv_ref[page] for page in ids], axis=0)
        return keys, values

    key_index = lax.broadcasted_iota(jnp.int32, (rows, KEY_BLOCK), 1)
    full = length // KEY_BLOCK

    def full_block(index, carry):
        update(*cached_block(index), None)
        return carry

    lax.fori_loop(0, full, full_block, 0)

    @pl.when(length % KEY_BLOCK > 0)
    def _():
        update(*cached_block(full), key_index < length - full * KEY_BLOCK)

    row_index = lax.broadcasted_iota(jnp.int32, (rows, KEY_BLOCK), 0) + first_row

    def new_block(index, carry):
        at = pl.multiple_of(index * KEY_BLOCK, KEY_BLOCK)
        update(
            nk_ref[pl.ds(at, KEY_BLOCK), :],
            nv_ref[pl.ds(at, KEY_BLOCK), :],
            key_index + at <= row_index,
        )
        return carry

    lax.fori_loop(0, (first_row + rows + KEY_BLOCK - 1) // KEY_BLOCK, new_block, 0)

    out = []
    for head in range(4):
        total = acc[head]
        mixed = total[:, :LANES] / total[:, LANES:]
        if head in (1, 2):
            mixed = pltpu.roll(mixed, HEAD_DIM, 1)
        out.append(mixed)
    o_ref[:, :LANES] = jnp.where(low, out[0], out[1]).astype(jnp.bfloat16)
    o_ref[:, LANES:] = jnp.where(low, out[2], out[3]).astype(jnp.bfloat16)


def out_kernel(att_ref, w_ref, x_ref, gain_ref, mid_ref, normed_ref):
    total = jnp.dot(att_ref[...], w_ref[...], preferred_element_type=jnp.float32)
    mid = (x_ref[...].astype(jnp.float32) + total).astype(jnp.bfloat16)
    mid_ref[...] = mid
    normed_ref[...] = rms_rows(mid.astype(jnp.float32), gain_ref[...])


def expert_kernel(first, last, x_ref, gates_ref, gu_ref, down_ref, *rest):
    before_ref, out_ref, total = (None, *rest) if first else rest
    expert = pl.program_id(1)
    rows = x_ref.shape[0]
    sub = min(rows, 256)
    gate_up = gu_ref[...].reshape(D, 2 * FF_EXPERT)
    down = down_ref[...].reshape(FF_EXPERT, D)

    def one(index, carry):
        span = pl.ds(pl.multiple_of(index * sub, sub), sub)
        both = jnp.dot(x_ref[span, :], gate_up, preferred_element_type=jnp.float32)
        lane = lax.broadcasted_iota(jnp.int32, (sub, gates_ref.shape[1]), 1)
        gate = jnp.sum(jnp.where(lane == expert, gates_ref[span, :], 0.0), axis=1, keepdims=True)
        left = both[:, :FF_EXPERT]
        act = left / (1.0 + jnp.exp(-left)) * both[:, FF_EXPERT:] * gate
        made = jnp.dot(act.astype(jnp.bfloat16), down, preferred_element_type=jnp.float32)

        @pl.when(expert == 0)
        def _():
            if first:
                total[span, :] = made
            else:
                total[span, :] = before_ref[span, :].astype(jnp.float32) + made

        @pl.when(expert > 0)
        def _():
            total[span, :] += made

        return carry

    lax.fori_loop(0, rows // sub, one, 0)

    @pl.when(expert == pl.num_programs(1) - 1)
    def _():
        out_ref[...] = total[...].astype(out_ref.dtype)


def experts(rows_in, gates, gate_up, down, before, last):
    total_rows = rows_in.shape[0]
    chunk = min(total_rows, 1024)
    tok, count, depth, _ = gate_up.shape
    ff_depth = down.shape[2]
    row_block = pl.BlockSpec((chunk, D), lambda r, e: (r, 0))
    in_specs = [
        row_block,
        pl.BlockSpec((chunk, gates.shape[1]), lambda r, e: (r, 0)),
        pl.BlockSpec((tok, 1, depth, 2 * FF_EXPERT), lambda r, e: (0, e, 0, 0)),
        pl.BlockSpec((tok, 1, ff_depth, D), lambda r, e: (0, e, 0, 0)),
    ]
    operands = [rows_in, gates, gate_up, down]
    if before is not None:
        in_specs.append(row_block)
        operands.append(before)
    kind = jnp.bfloat16 if last else jnp.float32
    return pl.pallas_call(
        functools.partial(expert_kernel, before is None, last),
        grid=(total_rows // chunk, count),
        in_specs=in_specs,
        out_specs=row_block,
        out_shape=jax.ShapeDtypeStruct((total_rows, D), kind),
        scratch_shapes=[pltpu.VMEM((chunk, D), jnp.float32)],
        compiler_params=params("arbitrary", "arbitrary"),
        cost_estimate=pl.CostEstimate(
            flops=6 * total_rows * count * D * FF_EXPERT,
            bytes_accessed=2 * (gate_up.size + down.size) * (total_rows // chunk)
            + 8 * total_rows * D,
            transcendentals=total_rows * count * FF_EXPERT,
        ),
    )(*operands)


def shards(
    hidden_states,
    first_gain,
    second_gain,
    w_query,
    w_keyval,
    w_out,
    kv_cache,
    page_table,
    cached_len,
    expert_ids,
    gate_weights,
    w_gate_up,
    w_down,
):
    rows = hidden_states.shape[0]
    tp_size = lax.axis_size("tp")
    tp_rank = lax.axis_index("tp")
    per_request = tp_size // REQ_DEV
    request = tp_rank // per_request
    first_row = (tp_rank % per_request) * rows
    bf16 = jnp.bfloat16

    query_full = lax.all_gather(w_query, "tp", axis=1, tiled=True)
    out_full = lax.all_gather(w_out, "tp", axis=0, tiled=True)
    local = EXPERTS // tp_size
    step = max(local // EXPERT_GROUPS, 1)
    gathered = [
        (
            lax.all_gather(w_gate_up[at : at + step], "tok", axis=0),
            lax.all_gather(w_down[at : at + step], "tok", axis=0),
        )
        for at in range(0, local, step)
    ]

    expert_range = jnp.arange(EXPERTS, dtype=jnp.int32)
    dense = jnp.sum(
        jnp.where(
            expert_ids[:, :, None] == expert_range[None, None, :], gate_weights[:, :, None], 0.0
        ),
        axis=1,
    )
    dense = lax.all_gather(dense, "tp", axis=0, tiled=True)
    gates = lax.dynamic_slice_in_dim(dense, tp_rank * local, local, 1)

    length = jnp.sum(jnp.where(jnp.arange(REQ_DEV) == request, cached_len, 0))
    pages = jnp.sum(
        jnp.where(jnp.arange(REQ_DEV)[:, None] == request, page_table, 0), axis=0
    ) - lax.axis_index("tok") * kv_cache.shape[0]
    positions = (length + first_row + jnp.arange(rows, dtype=jnp.int32)).astype(jnp.float32)
    half = HEAD_DIM // 2
    frequency = jnp.power(THETA, -(jnp.arange(half).astype(jnp.float32) * (2.0 / HEAD_DIM)))
    angles = positions[:, None] * frequency[None, :]
    cosine, sine = jnp.cos(angles), jnp.sin(angles)
    cosine = jnp.concatenate([cosine] * 4, axis=1)
    sine = jnp.concatenate([-sine, sine, -sine, sine], axis=1)

    normed, keyval = pl.pallas_call(
        keyval_kernel,
        out_shape=(jax.ShapeDtypeStruct((rows, D), bf16), jax.ShapeDtypeStruct((rows, D), bf16)),
        compiler_params=params(),
        cost_estimate=pl.CostEstimate(
            flops=2 * rows * D * D, bytes_accessed=2 * D * D + 6 * rows * D, transcendentals=0
        ),
    )(hidden_states, first_gain.reshape(1, D), w_keyval, cosine, sine)
    groups = [
        [r * per_request + i for i in range(per_request)] for r in range(REQ_DEV)
    ]
    new_kv = lax.all_gather(keyval, "tp", axis=0, tiled=True, axis_index_groups=groups)
    queries = pl.pallas_call(
        query_kernel,
        out_shape=jax.ShapeDtypeStruct((rows, D), bf16),
        compiler_params=params(),
        cost_estimate=pl.CostEstimate(
            flops=2 * rows * D * D, bytes_accessed=2 * D * D + 4 * rows * D, transcendentals=0
        ),
    )(normed, query_full, cosine, sine)

    pool = kv_cache.shape[0]
    attended = pl.pallas_call(
        attention_kernel,
        grid_spec=pltpu.PrefetchScalarGridSpec(
            num_scalar_prefetch=2,
            grid=(PAIRS,),
            in_specs=[
                pl.BlockSpec((rows, 2 * LANES), lambda p, *_: (0, p)),
                pl.BlockSpec((pool, PAGE, LANES), lambda p, *_: (0, 0, p)),
                pl.BlockSpec((pool, PAGE, LANES), lambda p, *_: (0, 0, PAIRS + p)),
                pl.BlockSpec((NEW, LANES), lambda p, *_: (0, p)),
                pl.BlockSpec((NEW, LANES), lambda p, *_: (0, PAIRS + p)),
            ],
            out_specs=pl.BlockSpec((rows, 2 * LANES), lambda p, *_: (0, p)),
            scratch_shapes=[
                pltpu.VMEM((4, rows, LANES), bf16),
                pltpu.VMEM((4, rows, 1), jnp.float32),
                pltpu.VMEM((4, rows, 2 * LANES), jnp.float32),
            ],
        ),
        out_shape=jax.ShapeDtypeStruct((rows, D), bf16),
        compiler_params=params("arbitrary"),
        cost_estimate=pl.CostEstimate(
            flops=16 * rows * 3072 * D, bytes_accessed=12 * 1024 * 1024, transcendentals=rows * 3072 * 16
        ),
    )(pages, jnp.stack([length, first_row]).astype(jnp.int32), queries, kv_cache, kv_cache, new_kv, new_kv)

    middle, normed_two = pl.pallas_call(
        out_kernel,
        out_shape=(jax.ShapeDtypeStruct((rows, D), bf16), jax.ShapeDtypeStruct((rows, D), bf16)),
        compiler_params=params(),
        cost_estimate=pl.CostEstimate(
            flops=2 * rows * D * D, bytes_accessed=2 * D * D + 8 * rows * D, transcendentals=0
        ),
    )(attended, out_full, hidden_states, second_gain.reshape(1, D))

    rows_in = lax.all_gather(normed_two, "tp", axis=0, tiled=True)
    total = None
    for index, (gate_up, down) in enumerate(gathered):
        last = index == len(gathered) - 1
        part = gates[:, index * step : (index + 1) * step]
        total = experts(rows_in, part, gate_up, down, total, last)
    returned = lax.all_to_all(
        total.reshape(tp_size, rows, D), "tp", split_axis=0, concat_axis=0, tiled=True
    )
    mixture = jnp.sum(returned.astype(jnp.float32), axis=0)
    return (middle.astype(jnp.float32) + mixture).astype(bf16)


def solution(mesh):
    in_specs = (
        P(("tok", "tp"), None),
        P(),
        P(),
        P(None, "tp"),
        P(),
        P("tp", None),
        P("tok", None, None),
        P("tok", None),
        P("tok"),
        P(("tok", "tp"), None),
        P(("tok", "tp"), None),
        P("tp", "tok", None),
        P("tp", "tok", None),
    )
    out_specs = P(("tok", "tp"), None)
    return jax.shard_map(shards, mesh=mesh, in_specs=in_specs, out_specs=out_specs, check_vma=False)
```

```python
import functools

import jax
import jax.numpy as jnp
from jax import lax
from jax.experimental import pallas as pl
from jax.experimental.pallas import tpu as pltpu
from jax.sharding import PartitionSpec as P

D = 1024
HEADS = 16
KV_HEADS = 8
HEAD_DIM = 64
EXPERTS = 32
FF_EXPERT = 512
TOP = 8
NEW = 1024
REQ_DEV = 2
PAGE = 128
MAX_PAGES = 16

ATTN_SCALE = 0.015625
EPSILON = 1e-06
THETA = 10000.0

LANES = 128
PAIRS = KV_HEADS // 2
KEY_BLOCK = 512
EXPERT_GROUPS = 4
NEGATIVE = -1e30
VMEM_LIMIT = 56 * 1024 * 1024


def params(*semantics):
    return pltpu.CompilerParams(
        vmem_limit_bytes=VMEM_LIMIT, dimension_semantics=semantics or None
    )


def rms_rows(wide, gain):
    factor = lax.rsqrt(jnp.mean(wide * wide, axis=-1, keepdims=True) + EPSILON)
    return (wide * factor * gain).astype(jnp.bfloat16)


def turn(values, cosine, sine):
    lane = lax.broadcasted_iota(jnp.int32, values.shape, 1)
    partner = jnp.where(
        lane % HEAD_DIM < HEAD_DIM // 2, pltpu.roll(values, 96, 1), pltpu.roll(values, 32, 1)
    )
    return values * cosine + partner * sine


def keyval_kernel(x_ref, gain_ref, w_ref, cos_ref, sin_ref, normed_ref, kv_ref):
    normed = rms_rows(x_ref[...].astype(jnp.float32), gain_ref[...])
    normed_ref[...] = normed
    for at in range(0, D, 256):
        part = jnp.dot(normed, w_ref[:, at : at + 256], preferred_element_type=jnp.float32)
        for sub in range(0, 256, LANES):
            piece = part[:, sub : sub + LANES]
            if at < KV_HEADS * HEAD_DIM:
                piece = turn(piece, cos_ref[...], sin_ref[...])
            kv_ref[:, at + sub : at + sub + LANES] = piece.astype(jnp.bfloat16)


def query_kernel(normed_ref, w_ref, cos_ref, sin_ref, q_ref):
    normed = normed_ref[...]
    for at in range(0, D, 256):
        part = jnp.dot(normed, w_ref[:, at : at + 256], preferred_element_type=jnp.float32)
        for sub in range(0, 256, LANES):
            piece = turn(part[:, sub : sub + LANES], cos_ref[...], sin_ref[...])
            piece = piece.astype(jnp.bfloat16).astype(jnp.float32) * ATTN_SCALE
            q_ref[:, at + sub : at + sub + LANES] = piece.astype(jnp.bfloat16)


def attention_kernel(
    pages_ref, sizes_ref, q_ref, ck_ref, cv_ref, nk_ref, nv_ref, o_ref, qp, top, acc
):
    rows = q_ref.shape[0]
    length = sizes_ref[0]
    first_row = sizes_ref[1]
    lane = lax.broadcasted_iota(jnp.int32, (rows, LANES), 1)
    low = lane < HEAD_DIM
    for head in range(4):
        block = q_ref[:, (head // 2) * LANES : (head // 2 + 1) * LANES].astype(jnp.float32)
        if head in (1, 2):
            block = pltpu.roll(block, HEAD_DIM, 1)
        keep = low if head < 2 else jnp.logical_not(low)
        qp[head] = jnp.where(keep, block, 0.0).astype(jnp.bfloat16)
        top[head] = jnp.full((rows, 1), NEGATIVE, jnp.float32)
        acc[head] = jnp.zeros((rows, 2 * LANES), jnp.float32)

    def update(keys, values, allowed):
        extended = jnp.concatenate([values, jnp.ones_like(values)], axis=1)
        for head in range(4):
            scores = lax.dot_general(
                qp[head], keys, (((1,), (1,)), ((), ())), preferred_element_type=jnp.float32
            )
            if allowed is not None:
                scores = jnp.where(allowed, scores, NEGATIVE)
            before = top[head]
            after = jnp.maximum(before, jnp.max(scores, axis=1, keepdims=True))
            weights = jnp.exp(scores - after).astype(jnp.bfloat16)
            top[head] = after
            acc[head] = acc[head] * jnp.exp(before - after) + jnp.dot(
                weights, extended, preferred_element_type=jnp.float32
            )

    per_block = KEY_BLOCK // PAGE

    def cached_block(index):
        ids = [pages_ref[index * per_block + i] for i in range(per_block)]
        keys = jnp.concatenate([ck_ref[page] for page in ids], axis=0)
        values = jnp.concatenate([cv_ref[page] for page in ids], axis=0)
        return keys, values

    key_index = lax.broadcasted_iota(jnp.int32, (rows, KEY_BLOCK), 1)
    full = length // KEY_BLOCK

    def full_block(index, carry):
        update(*cached_block(index), None)
        return carry

    lax.fori_loop(0, full, full_block, 0)

    @pl.when(length % KEY_BLOCK > 0)
    def _():
        update(*cached_block(full), key_index < length - full * KEY_BLOCK)

    row_index = lax.broadcasted_iota(jnp.int32, (rows, KEY_BLOCK), 0) + first_row

    def new_block(index, carry):
        at = pl.multiple_of(index * KEY_BLOCK, KEY_BLOCK)
        update(
            nk_ref[pl.ds(at, KEY_BLOCK), :],
            nv_ref[pl.ds(at, KEY_BLOCK), :],
            key_index + at <= row_index,
        )
        return carry

    lax.fori_loop(0, (first_row + rows + KEY_BLOCK - 1) // KEY_BLOCK, new_block, 0)

    out = []
    for head in range(4):
        total = acc[head]
        mixed = total[:, :LANES] / total[:, LANES:]
        if head in (1, 2):
            mixed = pltpu.roll(mixed, HEAD_DIM, 1)
        out.append(mixed)
    o_ref[:, :LANES] = jnp.where(low, out[0], out[1]).astype(jnp.bfloat16)
    o_ref[:, LANES:] = jnp.where(low, out[2], out[3]).astype(jnp.bfloat16)


def out_kernel(att_ref, w_ref, x_ref, gain_ref, mid_ref, normed_ref):
    total = jnp.dot(att_ref[...], w_ref[...], preferred_element_type=jnp.float32)
    mid = (x_ref[...].astype(jnp.float32) + total).astype(jnp.bfloat16)
    mid_ref[...] = mid
    normed_ref[...] = rms_rows(mid.astype(jnp.float32), gain_ref[...])


def expert_kernel(first, last, x_ref, gates_ref, gu_ref, down_ref, *rest):
    before_ref, out_ref, total = (None, *rest) if first else rest
    expert = pl.program_id(1)
    rows = x_ref.shape[0]
    sub = min(rows, 256)
    gate_up = gu_ref[...].reshape(D, 2 * FF_EXPERT)
    down = down_ref[...].reshape(FF_EXPERT, D)

    def one(index, carry):
        span = pl.ds(pl.multiple_of(index * sub, sub), sub)
        both = jnp.dot(x_ref[span, :], gate_up, preferred_element_type=jnp.float32)
        lane = lax.broadcasted_iota(jnp.int32, (sub, gates_ref.shape[1]), 1)
        gate = jnp.sum(jnp.where(lane == expert, gates_ref[span, :], 0.0), axis=1, keepdims=True)
        left = both[:, :FF_EXPERT]
        act = left / (1.0 + jnp.exp(-left)) * both[:, FF_EXPERT:] * gate
        made = jnp.dot(act.astype(jnp.bfloat16), down, preferred_element_type=jnp.float32)

        @pl.when(expert == 0)
        def _():
            if first:
                total[span, :] = made
            else:
                total[span, :] = before_ref[span, :].astype(jnp.float32) + made

        @pl.when(expert > 0)
        def _():
            total[span, :] += made

        return carry

    lax.fori_loop(0, rows // sub, one, 0)

    @pl.when(expert == pl.num_programs(1) - 1)
    def _():
        out_ref[...] = total[...].astype(out_ref.dtype)


def experts(rows_in, gates, gate_up, down, before, last):
    total_rows = rows_in.shape[0]
    chunk = min(total_rows, 1024)
    tok, count, depth, _ = gate_up.shape
    ff_depth = down.shape[2]
    row_block = pl.BlockSpec((chunk, D), lambda r, e: (r, 0))
    in_specs = [
        row_block,
        pl.BlockSpec((chunk, gates.shape[1]), lambda r, e: (r, 0)),
        pl.BlockSpec((tok, 1, depth, 2 * FF_EXPERT), lambda r, e: (0, e, 0, 0)),
        pl.BlockSpec((tok, 1, ff_depth, D), lambda r, e: (0, e, 0, 0)),
    ]
    operands = [rows_in, gates, gate_up, down]
    if before is not None:
        in_specs.append(row_block)
        operands.append(before)
    kind = jnp.bfloat16 if last else jnp.float32
    return pl.pallas_call(
        functools.partial(expert_kernel, before is None, last),
        grid=(total_rows // chunk, count),
        in_specs=in_specs,
        out_specs=row_block,
        out_shape=jax.ShapeDtypeStruct((total_rows, D), kind),
        scratch_shapes=[pltpu.VMEM((chunk, D), jnp.float32)],
        compiler_params=params("arbitrary", "arbitrary"),
        cost_estimate=pl.CostEstimate(
            flops=6 * total_rows * count * D * FF_EXPERT,
            bytes_accessed=2 * (gate_up.size + down.size) * (total_rows // chunk)
            + 8 * total_rows * D,
            transcendentals=total_rows * count * FF_EXPERT,
        ),
    )(*operands)


def exchange(block, shift, size):
    return lax.ppermute(block, "tp", [(i, i ^ shift) for i in range(size)])


def collect(block, axis, count, size):
    width = block.shape[axis]
    place = lax.axis_index("tp") % count
    shape = list(block.shape)
    shape[axis] = width * count
    whole = jnp.zeros(shape, block.dtype)
    for shift in range(count):
        piece = block if shift == 0 else exchange(block, shift, size)
        owner = jnp.bitwise_xor(place, shift)
        whole = lax.dynamic_update_slice_in_dim(whole, piece, owner * width, axis)
    return whole


def shards(
    hidden_states,
    first_gain,
    second_gain,
    w_query,
    w_keyval,
    w_out,
    kv_cache,
    page_table,
    cached_len,
    expert_ids,
    gate_weights,
    w_gate_up,
    w_down,
):
    rows = hidden_states.shape[0]
    tp_size = lax.axis_size("tp")
    tp_rank = lax.axis_index("tp")
    per_request = tp_size // REQ_DEV
    request = tp_rank // per_request
    first_row = (tp_rank % per_request) * rows
    bf16 = jnp.bfloat16

    query_full = collect(w_query, 1, tp_size, tp_size)
    out_full = collect(w_out, 0, tp_size, tp_size)
    local = EXPERTS // tp_size
    step = max(local // EXPERT_GROUPS, 1)
    gathered = [
        (
            lax.all_gather(w_gate_up[at : at + step], "tok", axis=0),
            lax.all_gather(w_down[at : at + step], "tok", axis=0),
        )
        for at in range(0, local, step)
    ]

    expert_range = jnp.arange(EXPERTS, dtype=jnp.int32)
    dense = jnp.sum(
        jnp.where(
            expert_ids[:, :, None] == expert_range[None, None, :], gate_weights[:, :, None], 0.0
        ),
        axis=1,
    )
    gates = [
        lax.dynamic_slice_in_dim(
            exchange(dense, shift, tp_size) if shift else dense, tp_rank * local, local, 1
        )
        for shift in range(tp_size)
    ]

    length = jnp.sum(jnp.where(jnp.arange(REQ_DEV) == request, cached_len, 0))
    pages = jnp.sum(
        jnp.where(jnp.arange(REQ_DEV)[:, None] == request, page_table, 0), axis=0
    ) - lax.axis_index("tok") * kv_cache.shape[0]
    positions = (length + first_row + jnp.arange(rows, dtype=jnp.int32)).astype(jnp.float32)
    half = HEAD_DIM // 2
    frequency = jnp.power(THETA, -(jnp.arange(half).astype(jnp.float32) * (2.0 / HEAD_DIM)))
    angles = positions[:, None] * frequency[None, :]
    cosine, sine = jnp.cos(angles), jnp.sin(angles)
    cosine = jnp.concatenate([cosine] * 4, axis=1)
    sine = jnp.concatenate([-sine, sine, -sine, sine], axis=1)

    normed, keyval = pl.pallas_call(
        keyval_kernel,
        out_shape=(jax.ShapeDtypeStruct((rows, D), bf16), jax.ShapeDtypeStruct((rows, D), bf16)),
        compiler_params=params(),
        cost_estimate=pl.CostEstimate(
            flops=2 * rows * D * D, bytes_accessed=2 * D * D + 6 * rows * D, transcendentals=0
        ),
    )(hidden_states, first_gain.reshape(1, D), w_keyval, cosine, sine)
    new_kv = collect(keyval, 0, per_request, tp_size)
    queries = pl.pallas_call(
        query_kernel,
        out_shape=jax.ShapeDtypeStruct((rows, D), bf16),
        compiler_params=params(),
        cost_estimate=pl.CostEstimate(
            flops=2 * rows * D * D, bytes_accessed=2 * D * D + 4 * rows * D, transcendentals=0
        ),
    )(normed, query_full, cosine, sine)

    pool = kv_cache.shape[0]
    attended = pl.pallas_call(
        attention_kernel,
        grid_spec=pltpu.PrefetchScalarGridSpec(
            num_scalar_prefetch=2,
            grid=(PAIRS,),
            in_specs=[
                pl.BlockSpec((rows, 2 * LANES), lambda p, *_: (0, p)),
                pl.BlockSpec((pool, PAGE, LANES), lambda p, *_: (0, 0, p)),
                pl.BlockSpec((pool, PAGE, LANES), lambda p, *_: (0, 0, PAIRS + p)),
                pl.BlockSpec((NEW, LANES), lambda p, *_: (0, p)),
                pl.BlockSpec((NEW, LANES), lambda p, *_: (0, PAIRS + p)),
            ],
            out_specs=pl.BlockSpec((rows, 2 * LANES), lambda p, *_: (0, p)),
            scratch_shapes=[
                pltpu.VMEM((4, rows, LANES), bf16),
                pltpu.VMEM((4, rows, 1), jnp.float32),
                pltpu.VMEM((4, rows, 2 * LANES), jnp.float32),
            ],
        ),
        out_shape=jax.ShapeDtypeStruct((rows, D), bf16),
        compiler_params=params("arbitrary"),
        cost_estimate=pl.CostEstimate(
            flops=16 * rows * 3072 * D, bytes_accessed=12 * 1024 * 1024, transcendentals=rows * 3072 * 16
        ),
    )(pages, jnp.stack([length, first_row]).astype(jnp.int32), queries, kv_cache, kv_cache, new_kv, new_kv)

    middle, normed_two = pl.pallas_call(
        out_kernel,
        out_shape=(jax.ShapeDtypeStruct((rows, D), bf16), jax.ShapeDtypeStruct((rows, D), bf16)),
        compiler_params=params(),
        cost_estimate=pl.CostEstimate(
            flops=2 * rows * D * D, bytes_accessed=2 * D * D + 8 * rows * D, transcendentals=0
        ),
    )(attended, out_full, hidden_states, second_gain.reshape(1, D))

    shifts = list(range(tp_size))
    rows_in = [exchange(normed_two, shift, tp_size) if shift else normed_two for shift in shifts]
    totals = [None] * tp_size
    returned = [None] * tp_size
    for index, (gate_up, down) in enumerate(gathered):
        last = index == len(gathered) - 1
        span = slice(index * step, (index + 1) * step)
        for shift in reversed(shifts) if last else shifts:
            totals[shift] = experts(
                rows_in[shift], gates[shift][:, span], gate_up, down, totals[shift], last
            )
            if last:
                made = totals[shift]
                returned[shift] = exchange(made, shift, tp_size) if shift else made
        if not last:
            totals = list(lax.optimization_barrier(tuple(totals)))
    mixture = sum(part.astype(jnp.float32) for part in returned)
    return (middle.astype(jnp.float32) + mixture).astype(bf16)


def solution(mesh):
    in_specs = (
        P(("tok", "tp"), None),
        P(),
        P(),
        P(None, "tp"),
        P(),
        P("tp", None),
        P("tok", None, None),
        P("tok", None),
        P("tok"),
        P(("tok", "tp"), None),
        P(("tok", "tp"), None),
        P("tp", "tok", None),
        P("tp", "tok", None),
    )
    out_specs = P(("tok", "tp"), None)
    return jax.shard_map(shards, mesh=mesh, in_specs=in_specs, out_specs=out_specs, check_vma=False)
```
